32 devices in a mesh: groups: 2 (over x), ctx: 16 (over z, y, core).
Axes of the slice: x: 2, y: 2, z: 4, core: 2. Of those that a mesh axis runs over, the one named last changes fastest.
Arguments:
- tokens: bfloat16 [16384, 1024], P(('groups', 'ctx')), parts along dimension 0, may hold values from -24 to 24
- qkv_weight: bfloat16 [2048, 3072], P('groups'), parts along dimension 0, may hold values from -1 to 1
- out_grad: bfloat16 [16384, 1024], P(('groups', 'ctx')), parts along dimension 0, may hold values from -6 to 6
Outputs:
- token_grad: bfloat16 [16384, 1024], P(('groups', 'ctx')), parts along dimension 0
- weight_grad: float32 [2048, 3072], P(('groups', 'ctx')), parts along dimension 0
The draws below stay inside these ranges and needn't reach their ends.
There are 2 independent parts, one for each index of `groups`. The reference program is written for one: setup_inputs(seed, part) draws one part's arguments, and reference() takes and returns one part's arrays. A program takes and returns all parts, laid end to end along the dimension named above; each array names one. Nothing has to cross between parts.
All inputs are finite; a program needn't handle non-finite values.
Results may differ from the reference program's by a relative error of at most 0.03.
Values may be sent and summed in bfloat16 or wider, within the bound.
A program may use at most 128 MiB of HBM per device.

```python
import jax
import jax.numpy as jnp
from jax import lax

D = 1024
HEADS = 8
HEAD_DIM = 128
TOK_DEV = 512
TOKENS = 8192
N_CTX = 16


def draw_tokens(key, part):
    drawn = jnp.clip(jax.random.normal(key, (TOKENS, D), jnp.float32), -4.0, 4.0)
    return drawn.astype(jnp.bfloat16)


def draw_qkv_weight(key, part):
    factor = float(D) ** (-0.5)
    w_query = jnp.clip(jax.random.normal(jax.random.fold_in(key, 1), (D, D), jnp.float32), -5.0, 5.0) * factor
    w_keys = jnp.clip(jax.random.normal(jax.random.fold_in(key, 2), (D, D), jnp.float32), -5.0, 5.0) * factor
    w_values = jnp.clip(jax.random.normal(jax.random.fold_in(key, 3), (D, D), jnp.float32), -5.0, 5.0) * factor
    return jnp.concatenate([w_query, w_keys, w_values], axis=1).astype(jnp.bfloat16)


def shard_levels(own_key, dims, cuts, least, high):
    def one(axis_at, blocks):
        steps = jax.random.uniform(jax.random.fold_in(jax.random.fold_in(own_key, 6), axis_at), (blocks,), jnp.float32, least / len(cuts), high / len(cuts))
        return jnp.repeat(jnp.exp(steps), dims[axis_at] // blocks).reshape((-1,) + (1,) * (len(dims) - axis_at - 1))

    loudness = one(*cuts[0])
    for cut in cuts[1:]:
        loudness = loudness * one(*cut)
    return loudness


def noise(key, shape, width, most, shards=(), kind=jnp.bfloat16):
    result = width * jax.random.normal(key, shape, jnp.float32)
    if shards:
        result = result * shard_levels(key, shape, shards, -0.22, 0.18)
    return jnp.clip(result, -most, most).astype(kind)


def setup_inputs(seed: int = 0, part: int = 0) -> dict:
    arg_keys = jax.random.split(jax.random.key(seed), 4)
    own_keys = jax.random.split(jax.random.fold_in(arg_keys[3], part), 4)
    tokens = draw_tokens(jax.random.fold_in(jax.random.fold_in(arg_keys[3], part), 71), part)
    qkv_weight = draw_qkv_weight(jax.random.fold_in(jax.random.fold_in(arg_keys[3], part), 71), part)
    out_grad = noise(own_keys[2], (TOKENS, D), 1.0, 6.0, ((0, 16),))
    return dict(tokens=tokens, qkv_weight=qkv_weight, out_grad=out_grad)


def head_split(array):
    return array.reshape(array.shape[0], HEADS, HEAD_DIM).transpose(1, 0, 2)


def head_join(array):
    return array.transpose(1, 0, 2).reshape(array.shape[1], HEADS * HEAD_DIM)


def reference(tokens, qkv_weight, out_grad):
    qkv = jnp.dot(tokens, qkv_weight, preferred_element_type=jnp.float32).astype(jnp.bfloat16)
    query_all = qkv[:, :D].reshape(N_CTX, TOK_DEV, D)
    keys_all = qkv[:, D:2 * D].reshape(N_CTX, TOK_DEV, D)
    values_all = qkv[:, 2 * D:].reshape(N_CTX, TOK_DEV, D)
    grad_all = out_grad.reshape(N_CTX, TOK_DEV, D)
    score_scale = float(HEAD_DIM) ** -0.5

    def block_grads(block_index):
        window_index = ((block_index + jnp.arange(3, dtype=jnp.int32)) % N_CTX).astype(jnp.int32)
        keys_win = head_split(keys_all[window_index].reshape(3 * TOK_DEV, D)).astype(jnp.float32)
        values_win = head_split(values_all[window_index].reshape(3 * TOK_DEV, D)).astype(jnp.float32)
        query_head = head_split(query_all[block_index]).astype(jnp.float32)
        grad_head = head_split(grad_all[block_index]).astype(jnp.float32)
        scores = jnp.einsum("htd,hsd->hts", query_head, keys_win) * score_scale
        row_peak = jnp.max(scores, axis=-1, keepdims=True)
        log_total = row_peak + jnp.log(jnp.sum(jnp.exp(scores - row_peak), axis=-1, keepdims=True))
        attn_prob = jnp.exp(scores - log_total)
        prob_low = lax.optimization_barrier(attn_prob.astype(jnp.bfloat16)).astype(jnp.float32)
        output = jnp.einsum("hts,hsd->htd", prob_low, values_win)
        row_delta = jnp.sum(grad_head * output, axis=-1, keepdims=True)
        grad_prob = jnp.einsum("htd,hsd->hts", grad_head, values_win)
        grad_score = attn_prob * (grad_prob - row_delta) * score_scale
        grad_score = lax.optimization_barrier(grad_score.astype(jnp.bfloat16)).astype(jnp.float32)
        grad_query = head_join(jnp.einsum("hts,hsd->htd", grad_score, keys_win))
        grad_keys = head_join(jnp.einsum("hts,htd->hsd", grad_score, query_head)).reshape(3, TOK_DEV, D)
        grad_values = head_join(jnp.einsum("hts,htd->hsd", prob_low, grad_head)).reshape(3, TOK_DEV, D)
        return grad_query, grad_keys, grad_values

    grad_query, keys_terms, values_terms = lax.map(block_grads, jnp.arange(N_CTX, dtype=jnp.int32))
    grad_keys = jnp.zeros((N_CTX, TOK_DEV, D), jnp.float32)
    grad_values = jnp.zeros((N_CTX, TOK_DEV, D), jnp.float32)
    for offset in range(3):
        grad_keys = grad_keys + jnp.roll(keys_terms[:, offset], offset, axis=0)
        grad_values = grad_values + jnp.roll(values_terms[:, offset], offset, axis=0)
    grads = jnp.concatenate([grad_query, grad_keys, grad_values], axis=-1).reshape(TOKENS, 3 * D).astype(jnp.bfloat16)
    token_grad = jnp.dot(grads, qkv_weight.T, preferred_element_type=jnp.float32).astype(jnp.bfloat16)
    weight_grad = jnp.dot(tokens.T, grads, preferred_element_type=jnp.float32)
    return token_grad, weight_grad
```

```python
import functools

import jax
import jax.numpy as jnp
from jax import lax
from jax.experimental import pallas as pl
from jax.experimental.pallas import tpu as pltpu
from jax.sharding import PartitionSpec as P

HEAD_DIM = 128
PER_CALL = 2
SPAN = PER_CALL * HEAD_DIM
SCALE = float(HEAD_DIM) ** (-0.5)
LOG2E = 1.4426950408889634
LN2 = 0.6931471805599453
QUERY_TILE = 256


def passed_along(array, axis, by):
    size = lax.axis_size(axis)
    return lax.ppermute(array, axis, [(i, (i + by) % size) for i in range(size)])


def contract(a, b, da, db):
    return lax.dot_general(a, b, (((da,), (db,)), ((), ())), preferred_element_type=jnp.float32)


def attend_kernel(*refs, n_alias):
    (q, g, k0, k1, k2, v0, v1, v2, x0, x1, x2) = refs[:11]
    (dq, dk, dv, wg, prob, gscore) = refs[11 + n_alias:]
    rows = q.shape[0]
    for h in range(PER_CALL):
        cols = pl.ds(h * HEAD_DIM, HEAD_DIM)
        keys = jnp.concatenate([k0[:, cols], k1[:, cols], k2[:, cols]], axis=0)
        values = jnp.concatenate([v0[:, cols], v1[:, cols], v2[:, cols]], axis=0)
        inverses = []
        for t in range(rows // QUERY_TILE):
            part = pl.ds(t * QUERY_TILE, QUERY_TILE)
            scores = contract(keys, q[part, cols], 1, 1)
            peak = jnp.max(scores, axis=0, keepdims=True)
            weight = jnp.exp2(scores - peak)
            inverse = 1.0 / jnp.sum(weight, axis=0, keepdims=True)
            prob[:, part] = weight.astype(jnp.bfloat16)
            grad_prob = contract(values, g[part, cols], 1, 1)
            delta = jnp.sum(weight * grad_prob, axis=0, keepdims=True) * inverse
            gscore[:, part] = (weight * (grad_prob - delta)).astype(jnp.bfloat16)
            inverses.append(inverse)
        inverse = jnp.concatenate(inverses, axis=1)
        column = jnp.broadcast_to(inverse, (HEAD_DIM, rows)).T
        q_scaled = (q[:, cols].astype(jnp.float32) * (column * LN2)).astype(jnp.bfloat16)
        g_scaled = (g[:, cols].astype(jnp.float32) * column).astype(jnp.bfloat16)
        dk[:, cols] = contract(gscore[...], q_scaled, 1, 0).astype(jnp.bfloat16)
        dv[:, cols] = contract(prob[...], g_scaled, 1, 0).astype(jnp.bfloat16)
        dq_t = contract(keys, gscore[...], 0, 0) * (inverse * SCALE)
        dq[:, cols] = dq_t.T.astype(jnp.bfloat16)
    wg[:, :SPAN] = contract(x0[...], dq[...], 0, 0).astype(jnp.bfloat16)
    for at, grad in ((SPAN, dk), (2 * SPAN, dv)):
        total = contract(x0[...], grad[:rows, :], 0, 0)
        total += contract(x1[...], grad[rows:2 * rows, :], 0, 0)
        total += contract(x2[...], grad[2 * rows:, :], 0, 0)
        wg[:, at:at + SPAN] = total.astype(jnp.bfloat16)


def attend_call(chunk, q, g, kvs, xs, carry):
    rows, width = q.shape
    blocks = width // SPAN
    whole = lambda i: (0, 0)
    col = lambda by: (lambda i: (0, chunk + by))
    once = pl.Buffered(1)
    block = lambda shape, index: pl.BlockSpec(shape, index, pipeline_mode=once)
    in_specs = [block((rows, SPAN), col(0))] * 2
    in_specs += [block((rows, SPAN), col(0))] * 3 + [block((rows, SPAN), col(blocks))] * 3
    in_specs += [block((rows, width), whole)] * 3
    in_specs += [pl.BlockSpec(memory_space=pl.ANY)] * len(carry)
    out_specs = [
        block((rows, SPAN), col(0)),
        block((3 * rows, SPAN), col(0)),
        block((3 * rows, SPAN), col(0)),
        block((width, 3 * SPAN), whole),
    ]
    out_shape = [
        jax.ShapeDtypeStruct((rows, width), jnp.bfloat16),
        jax.ShapeDtypeStruct((3 * rows, width), jnp.bfloat16),
        jax.ShapeDtypeStruct((3 * rows, width), jnp.bfloat16),
        jax.ShapeDtypeStruct((width, 3 * SPAN), jnp.bfloat16),
    ]
    flops = 2 * (5 * rows * 3 * rows * SPAN * 2 + 7 * rows * width * SPAN)
    return pl.pallas_call(
        functools.partial(attend_kernel, n_alias=len(carry)),
        grid=(1,),
        in_specs=in_specs,
        out_specs=out_specs,
        out_shape=out_shape,
        scratch_shapes=[pltpu.VMEM((3 * rows, rows), jnp.bfloat16)] * 2,
        input_output_aliases={11 + i: i for i in range(len(carry))},
        compiler_params=pltpu.CompilerParams(vmem_limit_bytes=48 * 1024 * 1024),
        cost_estimate=pl.CostEstimate(
            flops=flops, bytes_accessed=8 * 1024 * 1024, transcendentals=3 * rows * rows * PER_CALL
        ),
        name="attend",
    )(q, g, *kvs, *kvs, *xs, *carry)


def back_kernel(*refs):
    (grads, weights, out) = (refs[: (len(refs) - 1) // 2], refs[(len(refs) - 1) // 2 : -1], refs[-1])
    total = contract(grads[0][...], weights[0][...], 1, 1)
    for grad, weight in zip(grads[1:], weights[1:]):
        total += contract(grad[...], weight[...], 1, 1)
    out[...] = total.astype(out.dtype)


def back_call(block, dq, dk, dv, qkv_weight, kind):
    rows, width = dq.shape
    tile = 256
    arrays = ([dq] if block == 0 else []) + [dk, dv]
    row_at = [0] * (len(arrays) - 2) + [block, block]
    first = 3 - len(arrays)
    in_specs = [pl.BlockSpec((rows, width), lambda i, r=r: (r, 0)) for r in row_at]
    in_specs += [
        pl.BlockSpec((tile, width), lambda i, c=c: (i, c)) for c in range(first, 3)
    ]
    return pl.pallas_call(
        back_kernel,
        grid=(width // tile,),
        in_specs=in_specs,
        out_specs=pl.BlockSpec((rows, tile), lambda i: (0, i)),
        out_shape=jax.ShapeDtypeStruct((rows, width), kind),
        compiler_params=pltpu.CompilerParams(vmem_limit_bytes=40 * 1024 * 1024),
        cost_estimate=pl.CostEstimate(
            flops=2 * rows * width * width * len(arrays),
            bytes_accessed=8 * 1024 * 1024,
            transcendentals=0,
        ),
        name="back",
    )(*arrays, *([qkv_weight] * len(arrays)))


def on_device(tokens, qkv_weight, out_grad):
    width = tokens.shape[1]
    low = jnp.bfloat16
    next_one = passed_along(tokens, "ctx", -1)
    next_two = passed_along(next_one, "ctx", -1)
    xs = (tokens, next_one, next_two)
    query = (
        jnp.dot(tokens, qkv_weight[:, :width], preferred_element_type=jnp.float32)
        * (SCALE * LOG2E)
    ).astype(low)
    kvs = [
        jnp.dot(x, qkv_weight[:, width:], preferred_element_type=jnp.float32).astype(low)
        for x in xs
    ]
    carry = ()
    parts = []
    for chunk in range(width // SPAN):
        *carry, wg = attend_call(chunk, query, out_grad, kvs, xs, carry)
        parts.append(
            lax.psum_scatter(wg, "ctx", scatter_dimension=0, tiled=True).astype(jnp.float32)
        )
    far = back_call(2, *carry, qkv_weight, low)
    moved = passed_along(far, "ctx", 1)
    mid = back_call(1, *carry, qkv_weight, jnp.float32)
    moved = passed_along((moved.astype(jnp.float32) + mid).astype(low), "ctx", 1)
    own = back_call(0, *carry, qkv_weight, jnp.float32)
    token_grad = (moved.astype(jnp.float32) + own).astype(low)
    weight_grad = jnp.concatenate(
        [p[:, i * SPAN:(i + 1) * SPAN] for i in range(3) for p in parts], axis=1
    )
    return (token_grad, weight_grad)


def solution(mesh):
    in_specs = (P(("groups", "ctx"), None), P("groups", None), P(("groups", "ctx"), None))
    out_specs = (P(("groups", "ctx"), None), P(("groups", "ctx"), None))
    return jax.shard_map(
        on_device, mesh=mesh, in_specs=in_specs, out_specs=out_specs, check_vma=False
    )
```

```python
import functools

import jax
import jax.numpy as jnp
from jax import lax
from jax.experimental import pallas as pl
from jax.experimental.pallas import tpu as pltpu
from jax.sharding import PartitionSpec as P

HEAD_DIM = 128
PER_CALL = 2
SPAN = PER_CALL * HEAD_DIM
SCALE = float(HEAD_DIM) ** (-0.5)
LOG2E = 1.4426950408889634
LN2 = 0.6931471805599453
QUERY_TILE = 256


def passed_along(array, axis, by):
    size = lax.axis_size(axis)
    return lax.ppermute(array, axis, [(i, (i + by) % size) for i in range(size)])


def contract(a, b, da, db):
    return lax.dot_general(a, b, (((da,), (db,)), ((), ())), preferred_element_type=jnp.float32)


def reversed_bits(value, count):
    out = 0
    while count > 1:
        out = out * 2 + value % 2
        value //= 2
        count //= 2
    return out


def attend_kernel(*refs, n_alias, owners):
    (q, g, k0, k1, k2, v0, v1, v2, x0, x1, x2) = refs[:11]
    (dq, dk, dv, wg, prob, gscore) = refs[11 + n_alias:]
    rows = q.shape[0]
    for h in range(PER_CALL):
        cols = pl.ds(h * HEAD_DIM, HEAD_DIM)
        keys = jnp.concatenate([k0[:, cols], k1[:, cols], k2[:, cols]], axis=0)
        values = jnp.concatenate([v0[:, cols], v1[:, cols], v2[:, cols]], axis=0)
        inverses = []
        for t in range(rows // QUERY_TILE):
            part = pl.ds(t * QUERY_TILE, QUERY_TILE)
            scores = contract(keys, q[part, cols], 1, 1)
            peak = jnp.max(scores, axis=0, keepdims=True)
            weight = jnp.exp2(scores - peak)
            inverse = 1.0 / jnp.sum(weight, axis=0, keepdims=True)
            prob[:, part] = weight.astype(jnp.bfloat16)
            grad_prob = contract(values, g[part, cols], 1, 1)
            delta = jnp.sum(weight * grad_prob, axis=0, keepdims=True) * inverse
            gscore[:, part] = (weight * (grad_prob - delta)).astype(jnp.bfloat16)
            inverses.append(inverse)
        inverse = jnp.concatenate(inverses, axis=1)
        column = jnp.broadcast_to(inverse, (HEAD_DIM, rows)).T
        q_scaled = (q[:, cols].astype(jnp.float32) * (column * LN2)).astype(jnp.bfloat16)
        g_scaled = (g[:, cols].astype(jnp.float32) * column).astype(jnp.bfloat16)
        dk[:, cols] = contract(gscore[...], q_scaled, 1, 0).astype(jnp.bfloat16)
        dv[:, cols] = contract(prob[...], g_scaled, 1, 0).astype(jnp.bfloat16)
        dq_t = contract(keys, gscore[...], 0, 0) * (inverse * SCALE)
        dq[:, cols] = dq_t.T.astype(jnp.bfloat16)
    share = wg.shape[0] // owners

    def put(at, total):
        for owner in range(owners):
            to = reversed_bits(owner, owners) * share
            wg[to:to + share, at:at + SPAN] = total[owner * share:(owner + 1) * share]

    put(0, contract(x0[...], dq[...], 0, 0).astype(jnp.bfloat16))
    for at, grad in ((SPAN, dk), (2 * SPAN, dv)):
        total = contract(x0[...], grad[:rows, :], 0, 0)
        total += contract(x1[...], grad[rows:2 * rows, :], 0, 0)
        total += contract(x2[...], grad[2 * rows:, :], 0, 0)
        put(at, total.astype(jnp.bfloat16))


def exchange(terms, axis, bit):
    size = lax.axis_size(axis)
    rows = terms.shape[0] // 2
    mine = lax.rem(lax.div(lax.axis_index(axis), bit), 2)
    keep = lax.dynamic_slice_in_dim(terms, mine * rows, rows, 0)
    send = lax.dynamic_slice_in_dim(terms, (1 - mine) * rows, rows, 0)
    taken = lax.ppermute(send, axis, [(i, i ^ bit) for i in range(size)])
    total = keep.astype(jnp.float32) + taken.astype(jnp.float32)
    return total.astype(jnp.bfloat16) if 2 * bit < size else total


def attend_call(chunk, q, g, kvs, xs, carry, after):
    rows, width = q.shape
    blocks = width // SPAN
    whole = lambda i: (0, 0)
    col = lambda by: (lambda i: (0, chunk + by))
    once = pl.Buffered(1)
    block = lambda shape, index: pl.BlockSpec(shape, index, pipeline_mode=once)
    in_specs = [block((rows, SPAN), col(0))] * 2
    in_specs += [block((rows, SPAN), col(0))] * 3 + [block((rows, SPAN), col(blocks))] * 3
    in_specs += [block((rows, width), whole)] * 3
    in_specs += [pl.BlockSpec(memory_space=pl.ANY)] * (len(carry) + len(after))
    out_specs = [
        block((rows, SPAN), col(0)),
        block((3 * rows, SPAN), col(0)),
        block((3 * rows, SPAN), col(0)),
        block((width, 3 * SPAN), whole),
    ]
    out_shape = [
        jax.ShapeDtypeStruct((rows, width), jnp.bfloat16),
        jax.ShapeDtypeStruct((3 * rows, width), jnp.bfloat16),
        jax.ShapeDtypeStruct((3 * rows, width), jnp.bfloat16),
        jax.ShapeDtypeStruct((width, 3 * SPAN), jnp.bfloat16),
    ]
    flops = 2 * (5 * rows * 3 * rows * SPAN * 2 + 7 * rows * width * SPAN)
    return pl.pallas_call(
        functools.partial(
            attend_kernel, n_alias=len(carry) + len(after), owners=lax.axis_size("ctx")
        ),
        grid=(1,),
        in_specs=in_specs,
        out_specs=out_specs,
        out_shape=out_shape,
        scratch_shapes=[pltpu.VMEM((3 * rows, rows), jnp.bfloat16)] * 2,
        input_output_aliases={11 + i: i for i in range(len(carry))},
        compiler_params=pltpu.CompilerParams(vmem_limit_bytes=58 * 1024 * 1024),
        cost_estimate=pl.CostEstimate(
            flops=flops, bytes_accessed=8 * 1024 * 1024, transcendentals=3 * rows * rows * PER_CALL
        ),
        name="attend",
    )(q, g, *kvs, *kvs, *xs, *carry, *after)


def back_kernel(*refs, terms, added):
    grads, weights, out = refs[:terms], refs[terms:2 * terms], refs[-1]
    total = contract(grads[0][...], weights[0][...], 1, 1)
    for grad, weight in zip(grads[1:], weights[1:]):
        total += contract(grad[...], weight[...], 1, 1)
    if added:
        total += refs[2 * terms][...].astype(jnp.float32)
    out[...] = total.astype(out.dtype)


def back_call(block, dq, dk, dv, qkv_weight, kind, added, after):
    rows, width = dq.shape
    tile = 256
    arrays = ([dq] if block == 0 else []) + [dk, dv]
    row_at = [0] * (len(arrays) - 2) + [block, block]
    first = 3 - len(arrays)
    in_specs = [pl.BlockSpec((rows, width), lambda i, r=r: (r, 0)) for r in row_at]
    in_specs += [
        pl.BlockSpec((tile, width), lambda i, c=c: (i, c)) for c in range(first, 3)
    ]
    in_specs += [pl.BlockSpec((rows, tile), lambda i: (0, i))] * len(added)
    in_specs += [pl.BlockSpec(memory_space=pl.ANY)] * len(after)
    return pl.pallas_call(
        functools.partial(back_kernel, terms=len(arrays), added=len(added)),
        grid=(width // tile,),
        in_specs=in_specs,
        out_specs=pl.BlockSpec((rows, tile), lambda i: (0, i)),
        out_shape=jax.ShapeDtypeStruct((rows, width), kind),
        compiler_params=pltpu.CompilerParams(vmem_limit_bytes=58 * 1024 * 1024),
        cost_estimate=pl.CostEstimate(
            flops=2 * rows * width * width * len(arrays),
            bytes_accessed=8 * 1024 * 1024,
            transcendentals=0,
        ),
        name="back",
    )(*arrays, *([qkv_weight] * len(arrays)), *added, *after)


def on_device(tokens, qkv_weight, out_grad):
    width = tokens.shape[1]
    low = jnp.bfloat16
    next_one = passed_along(tokens, "ctx", -1)
    next_two = passed_along(next_one, "ctx", -1)
    xs = (tokens, next_one, next_two)
    query = (
        jnp.dot(tokens, qkv_weight[:, :width], preferred_element_type=jnp.float32)
        * (SCALE * LOG2E)
    ).astype(low)
    kvs = [
        jnp.dot(x, qkv_weight[:, width:], preferred_element_type=jnp.float32).astype(low)
        for x in xs
    ]
    bits = []
    while 2 ** len(bits) < lax.axis_size("ctx"):
        bits.append(2 ** len(bits))
    carry = ()
    sums = []
    done = []

    def advance():
        for i, total in enumerate(sums):
            if done[i] < len(bits):
                sums[i] = exchange(total, "ctx", bits[done[i]])
                done[i] += 1

    for chunk in range(width // SPAN):
        fresh = list(sums)
        *carry, wg = attend_call(chunk, query, out_grad, kvs, xs, carry, fresh)
        advance()
        sums.append(wg)
        done.append(0)
    far = back_call(2, *carry, qkv_weight, low, (), sums[:-1])
    moved = passed_along(far, "ctx", 1)
    advance()
    mid = back_call(1, *carry, qkv_weight, low, (moved,), sums[:-1])
    moved = passed_along(mid, "ctx", 1)
    advance()
    own = back_call(0, *carry, qkv_weight, jnp.float32, (), ())
    token_grad = (moved.astype(jnp.float32) + own).astype(low)
    while min(done) < len(bits):
        advance()
    parts = sums
    weight_grad = jnp.concatenate(
        [p[:, i * SPAN:(i + 1) * SPAN] for i in range(3) for p in parts], axis=1
    )
    return (token_grad, weight_grad)


def solution(mesh):
    in_specs = (P(("groups", "ctx"), None), P("groups", None), P(("groups", "ctx"), None))
    out_specs = (P(("groups", "ctx"), None), P(("groups", "ctx"), None))
    return jax.shard_map(
        on_device, mesh=mesh, in_specs=in_specs, out_specs=out_specs, check_vma=False
    )
```

```python
import functools

import jax
import jax.numpy as jnp
from jax import lax
from jax.experimental import pallas as pl
from jax.experimental.pallas import tpu as pltpu
from jax.sharding import PartitionSpec as P

HEAD_DIM = 128
PER_CALL = 2
SPAN = PER_CALL * HEAD_DIM
SCALE = float(HEAD_DIM) ** (-0.5)
LOG2E = 1.4426950408889634
LN2 = 0.6931471805599453
QUERY_TILE = 256


def passed_along(array, axis, by):
    size = lax.axis_size(axis)
    return lax.ppermute(array, axis, [(i, (i + by) % size) for i in range(size)])


def contract(a, b, da, db):
    return lax.dot_general(a, b, (((da,), (db,)), ((), ())), preferred_element_type=jnp.float32)


def reversed_bits(value, count):
    out = 0
    while count > 1:
        out = out * 2 + value % 2
        value //= 2
        count //= 2
    return out


def attend_kernel(*refs, n_alias, owners):
    (q, g, k0, k1, k2, v0, v1, v2, x0, x1, x2) = refs[:11]
    (dq, dk, dv, wg, prob, gscore) = refs[11 + n_alias:]
    rows = q.shape[0]
    for h in range(PER_CALL):
        cols = pl.ds(h * HEAD_DIM, HEAD_DIM)
        keys = jnp.concatenate([k0[:, cols], k1[:, cols], k2[:, cols]], axis=0)
        values = jnp.concatenate([v0[:, cols], v1[:, cols], v2[:, cols]], axis=0)
        inverses = []
        for t in range(rows // QUERY_TILE):
            part = pl.ds(t * QUERY_TILE, QUERY_TILE)
            scores = contract(keys, q[part, cols], 1, 1)
            peak = jnp.max(scores, axis=0, keepdims=True)
            weight = jnp.exp2(scores - peak)
            inverse = 1.0 / jnp.sum(weight, axis=0, keepdims=True)
            prob[:, part] = weight.astype(jnp.bfloat16)
            grad_prob = contract(values, g[part, cols], 1, 1)
            delta = jnp.sum(weight * grad_prob, axis=0, keepdims=True) * inverse
            gscore[:, part] = (weight * (grad_prob - delta)).astype(jnp.bfloat16)
            inverses.append(inverse)
        inverse = jnp.concatenate(inverses, axis=1)
        column = jnp.broadcast_to(inverse, (HEAD_DIM, rows)).T
        q_scaled = (q[:, cols].astype(jnp.float32) * (column * LN2)).astype(jnp.bfloat16)
        g_scaled = (g[:, cols].astype(jnp.float32) * column).astype(jnp.bfloat16)
        dk[:, cols] = contract(gscore[...], q_scaled, 1, 0).astype(jnp.bfloat16)
        dv[:, cols] = contract(prob[...], g_scaled, 1, 0).astype(jnp.bfloat16)
        dq_t = contract(keys, gscore[...], 0, 0) * (inverse * SCALE)
        dq[:, cols] = dq_t.T.astype(jnp.bfloat16)
    share = wg.shape[0] // owners

    def put(at, total):
        for owner in range(owners):
            to = reversed_bits(owner, owners) * share
            wg[to:to + share, at:at + SPAN] = total[owner * share:(owner + 1) * share]

    put(0, contract(x0[...], dq[...], 0, 0).astype(jnp.bfloat16))
    for at, grad in ((SPAN, dk), (2 * SPAN, dv)):
        total = contract(x0[...], grad[:rows, :], 0, 0)
        total += contract(x1[...], grad[rows:2 * rows, :], 0, 0)
        total += contract(x2[...], grad[2 * rows:, :], 0, 0)
        put(at, total.astype(jnp.bfloat16))


def exchange(terms, axis, bit):
    size = lax.axis_size(axis)
    rows = terms.shape[0] // 2
    mine = lax.rem(lax.div(lax.axis_index(axis), bit), 2)
    keep = lax.dynamic_slice_in_dim(terms, mine * rows, rows, 0)
    send = lax.dynamic_slice_in_dim(terms, (1 - mine) * rows, rows, 0)
    taken = lax.ppermute(send, axis, [(i, i ^ bit) for i in range(size)])
    total = keep.astype(jnp.float32) + taken.astype(jnp.float32)
    return total.astype(jnp.bfloat16) if 2 * bit < size else total


def attend_call(chunk, q, g, kvs, xs, carry, after):
    rows, width = q.shape
    blocks = width // SPAN
    whole = lambda i: (0, 0)
    col = lambda by: (lambda i: (0, chunk + by))
    once = pl.Buffered(1)
    block = lambda shape, index: pl.BlockSpec(shape, index, pipeline_mode=once)
    in_specs = [block((rows, SPAN), col(0))] * 2
    in_specs += [block((rows, SPAN), col(0))] * 3 + [block((rows, SPAN), col(blocks))] * 3
    in_specs += [block((rows, width), whole)] * 3
    in_specs += [pl.BlockSpec(memory_space=pl.ANY)] * (len(carry) + len(after))
    out_specs = [
        block((rows, SPAN), col(0)),
        block((3 * rows, SPAN), col(0)),
        block((3 * rows, SPAN), col(0)),
        block((width, 3 * SPAN), whole),
    ]
    out_shape = [
        jax.ShapeDtypeStruct((rows, width), jnp.bfloat16),
        jax.ShapeDtypeStruct((3 * rows, width), jnp.bfloat16),
        jax.ShapeDtypeStruct((3 * rows, width), jnp.bfloat16),
        jax.ShapeDtypeStruct((width, 3 * SPAN), jnp.bfloat16),
    ]
    flops = 2 * (5 * rows * 3 * rows * SPAN * 2 + 7 * rows * width * SPAN)
    return pl.pallas_call(
        functools.partial(
            attend_kernel, n_alias=len(carry) + len(after), owners=lax.axis_size("ctx")
        ),
        grid=(1,),
        in_specs=in_specs,
        out_specs=out_specs,
        out_shape=out_shape,
        scratch_shapes=[pltpu.VMEM((3 * rows, rows), jnp.bfloat16)] * 2,
        input_output_aliases={11 + i: i for i in range(len(carry))},
        compiler_params=pltpu.CompilerParams(vmem_limit_bytes=58 * 1024 * 1024),
        cost_estimate=pl.CostEstimate(
            flops=flops, bytes_accessed=8 * 1024 * 1024, transcendentals=3 * rows * rows * PER_CALL
        ),
        name="attend",
    )(q, g, *kvs, *kvs, *xs, *carry, *after)


def back_kernel(*refs, terms, added):
    grads, weights, out = refs[:terms], refs[terms:2 * terms], refs[-1]
    total = contract(grads[0][...], weights[0][...], 1, 1)
    for grad, weight in zip(grads[1:], weights[1:]):
        total += contract(grad[...], weight[...], 1, 1)
    if added:
        total += refs[2 * terms][...].astype(jnp.float32)
    out[...] = total.astype(out.dtype)


def back_call(block, dq, dk, dv, qkv_weight, kind, added, after):
    rows, width = dq.shape
    tile = 256
    arrays = ([dq] if block == 0 else []) + [dk, dv]
    row_at = [0] * (len(arrays) - 2) + [block, block]
    first = 3 - len(arrays)
    in_specs = [pl.BlockSpec((rows, width), lambda i, r=r: (r, 0)) for r in row_at]
    in_specs += [
        pl.BlockSpec((tile, width), lambda i, c=c: (i, c)) for c in range(first, 3)
    ]
    in_specs += [pl.BlockSpec((rows, tile), lambda i: (0, i))] * len(added)
    in_specs += [pl.BlockSpec(memory_space=pl.ANY)] * len(after)
    return pl.pallas_call(
        functools.partial(back_kernel, terms=len(arrays), added=len(added)),
        grid=(width // tile,),
        in_specs=in_specs,
        out_specs=pl.BlockSpec((rows, tile), lambda i: (0, i)),
        out_shape=jax.ShapeDtypeStruct((rows, width), kind),
        compiler_params=pltpu.CompilerParams(vmem_limit_bytes=58 * 1024 * 1024),
        cost_estimate=pl.CostEstimate(
            flops=2 * rows * width * width * len(arrays),
            bytes_accessed=8 * 1024 * 1024,
            transcendentals=0,
        ),
        name="back",
    )(*arrays, *([qkv_weight] * len(arrays)), *added, *after)


def on_device(tokens, qkv_weight, out_grad):
    width = tokens.shape[1]
    low = jnp.bfloat16
    next_one = passed_along(tokens, "ctx", -1)
    next_two = passed_along(next_one, "ctx", -1)
    xs = (tokens, next_one, next_two)
    query = (
        jnp.dot(tokens, qkv_weight[:, :width], preferred_element_type=jnp.float32)
        * (SCALE * LOG2E)
    ).astype(low)
    kvs = [
        jnp.dot(x, qkv_weight[:, width:], preferred_element_type=jnp.float32).astype(low)
        for x in xs
    ]
    bits = []
    while 2 ** len(bits) < lax.axis_size("ctx"):
        bits.append(2 ** len(bits))
    carry = ()
    sums = []
    done = []

    def advance():
        for i in range(len(sums)):
            if done[i] < len(bits):
                sums[i] = exchange(sums[i], "ctx", bits[done[i]])
                done[i] += 1

    for chunk in range(width // SPAN):
        fresh = list(sums)
        *carry, wg = attend_call(chunk, query, out_grad, kvs, xs, carry, fresh)
        advance()
        sums.append(wg)
        done.append(0)
    far = back_call(2, *carry, qkv_weight, low, (), ())
    moved = passed_along(far, "ctx", 1)
    sums[:] = lax.optimization_barrier((far, *sums))[1:]
    advance()
    mid = back_call(1, *carry, qkv_weight, low, (moved,), ())
    moved = passed_along(mid, "ctx", 1)
    sums[:] = lax.optimization_barrier((mid, *sums))[1:]
    advance()
    own = back_call(0, *carry, qkv_weight, jnp.float32, (), (far,))
    token_grad = (moved.astype(jnp.float32) + own).astype(low)
    while min(done) < len(bits):
        advance()
    parts = sums
    weight_grad = jnp.concatenate(
        [p[:, i * SPAN:(i + 1) * SPAN] for i in range(3) for p in parts], axis=1
    )
    return (token_grad, weight_grad)


def solution(mesh):
    in_specs = (P(("groups", "ctx"), None), P("groups", None), P(("groups", "ctx"), None))
    out_specs = (P(("groups", "ctx"), None), P(("groups", "ctx"), None))
    return jax.shard_map(
        on_device, mesh=mesh, in_specs=in_specs, out_specs=out_specs, check_vma=False
    )
```

```python
import functools

import jax
import jax.numpy as jnp
from jax import lax
from jax.experimental import pallas as pl
from jax.experimental.pallas import tpu as pltpu
from jax.sharding import PartitionSpec as P

HEAD_DIM = 128
PER_CALL = 2
SPAN = PER_CALL * HEAD_DIM
SCALE = float(HEAD_DIM) ** (-0.5)
LOG2E = 1.4426950408889634
LN2 = 0.6931471805599453
QUERY_TILE = 256


def passed_along(array, axis, by):
    size = lax.axis_size(axis)
    return lax.ppermute(array, axis, [(i, (i + by) % size) for i in range(size)])


def contract(a, b, da, db):
    return lax.dot_general(a, b, (((da,), (db,)), ((), ())), preferred_element_type=jnp.float32)


def reversed_bits(value, count):
    out = 0
    while count > 1:
        out = out * 2 + value % 2
        value //= 2
        count //= 2
    return out


def attend_kernel(*refs, n_alias, owners):
    (q, g, k0, k1, k2, v0, v1, v2, x0, x1, x2) = refs[:11]
    (dq, dk, dv, wg, prob, gscore) = refs[11 + n_alias:]
    rows = q.shape[0]
    for h in range(PER_CALL):
        cols = pl.ds(h * HEAD_DIM, HEAD_DIM)
        keys = jnp.concatenate([k0[:, cols], k1[:, cols], k2[:, cols]], axis=0)
        values = jnp.concatenate([v0[:, cols], v1[:, cols], v2[:, cols]], axis=0)
        inverses = []
        for t in range(rows // QUERY_TILE):
            part = pl.ds(t * QUERY_TILE, QUERY_TILE)
            scores = contract(keys, q[part, cols], 1, 1)
            peak = jnp.max(scores, axis=0, keepdims=True)
            weight = jnp.exp2(scores - peak)
            inverse = 1.0 / jnp.sum(weight, axis=0, keepdims=True)
            prob[:, part] = weight.astype(jnp.bfloat16)
            grad_prob = contract(values, g[part, cols], 1, 1)
            delta = jnp.sum(weight * grad_prob, axis=0, keepdims=True) * inverse
            gscore[:, part] = (weight * (grad_prob - delta)).astype(jnp.bfloat16)
            inverses.append(inverse)
        inverse = jnp.concatenate(inverses, axis=1)
        column = jnp.broadcast_to(inverse, (HEAD_DIM, rows)).T
        q_scaled = (q[:, cols].astype(jnp.float32) * (column * LN2)).astype(jnp.bfloat16)
        g_scaled = (g[:, cols].astype(jnp.float32) * column).astype(jnp.bfloat16)
        dk[:, cols] = contract(gscore[...], q_scaled, 1, 0).astype(jnp.bfloat16)
        dv[:, cols] = contract(prob[...], g_scaled, 1, 0).astype(jnp.bfloat16)
        dq_t = contract(keys, gscore[...], 0, 0) * (inverse * SCALE)
        dq[:, cols] = dq_t.T.astype(jnp.bfloat16)
    share = wg.shape[0] // owners

    def put(at, total):
        for owner in range(owners):
            to = reversed_bits(owner, owners) * share
            wg[to:to + share, at:at + SPAN] = total[owner * share:(owner + 1) * share]

    put(0, contract(x0[...], dq[...], 0, 0).astype(jnp.bfloat16))
    for at, grad in ((SPAN, dk), (2 * SPAN, dv)):
        total = contract(x0[...], grad[:rows, :], 0, 0)
        total += contract(x1[...], grad[rows:2 * rows, :], 0, 0)
        total += contract(x2[...], grad[2 * rows:, :], 0, 0)
        put(at, total.astype(jnp.bfloat16))


def exchange(terms, axis, bit):
    size = lax.axis_size(axis)
    rows = terms.shape[0] // 2
    mine = lax.rem(lax.div(lax.axis_index(axis), bit), 2)
    keep = lax.dynamic_slice_in_dim(terms, mine * rows, rows, 0)
    send = lax.dynamic_slice_in_dim(terms, (1 - mine) * rows, rows, 0)
    taken = lax.ppermute(send, axis, [(i, i ^ bit) for i in range(size)])
    total = keep.astype(jnp.float32) + taken.astype(jnp.float32)
    return total.astype(jnp.bfloat16) if 2 * bit < size else total


def attend_call(chunk, q, g, kvs, xs, carry, after):
    rows, width = q.shape
    blocks = width // SPAN
    whole = lambda i: (0, 0)
    col = lambda by: (lambda i: (0, chunk + by))
    once = pl.Buffered(1)
    block = lambda shape, index: pl.BlockSpec(shape, index, pipeline_mode=once)
    in_specs = [block((rows, SPAN), col(0))] * 2
    in_specs += [block((rows, SPAN), col(0))] * 3 + [block((rows, SPAN), col(blocks))] * 3
    in_specs += [block((rows, width), whole)] * 3
    in_specs += [pl.BlockSpec(memory_space=pl.ANY)] * (len(carry) + len(after))
    out_specs = [
        block((rows, SPAN), col(0)),
        block((3 * rows, SPAN), col(0)),
        block((3 * rows, SPAN), col(0)),
        block((width, 3 * SPAN), whole),
    ]
    out_shape = [
        jax.ShapeDtypeStruct((rows, width), jnp.bfloat16),
        jax.ShapeDtypeStruct((3 * rows, width), jnp.bfloat16),
        jax.ShapeDtypeStruct((3 * rows, width), jnp.bfloat16),
        jax.ShapeDtypeStruct((width, 3 * SPAN), jnp.bfloat16),
    ]
    flops = 2 * (5 * rows * 3 * rows * SPAN * 2 + 7 * rows * width * SPAN)
    return pl.pallas_call(
        functools.partial(
            attend_kernel, n_alias=len(carry) + len(after), owners=lax.axis_size("ctx")
        ),
        grid=(1,),
        in_specs=in_specs,
        out_specs=out_specs,
        out_shape=out_shape,
        scratch_shapes=[pltpu.VMEM((3 * rows, rows), jnp.bfloat16)] * 2,
        input_output_aliases={11 + i: i for i in range(len(carry))},
        compiler_params=pltpu.CompilerParams(vmem_limit_bytes=58 * 1024 * 1024),
        cost_estimate=pl.CostEstimate(
            flops=flops, bytes_accessed=8 * 1024 * 1024, transcendentals=3 * rows * rows * PER_CALL
        ),
        name="attend",
    )(q, g, *kvs, *kvs, *xs, *carry, *after)


def back_kernel(*refs, terms, added):
    grads, weights, out = refs[:terms], refs[terms:2 * terms], refs[-1]
    total = contract(grads[0][...], weights[0][...], 1, 1)
    for grad, weight in zip(grads[1:], weights[1:]):
        total += contract(grad[...], weight[...], 1, 1)
    if added:
        total += refs[2 * terms][...].astype(jnp.float32)
    out[...] = total.astype(out.dtype)


def back_call(block, dq, dk, dv, qkv_weight, kind, added, after):
    rows, width = dq.shape
    tile = 256
    arrays = ([dq] if block == 0 else []) + [dk, dv]
    row_at = [0] * (len(arrays) - 2) + [block, block]
    first = 3 - len(arrays)
    in_specs = [pl.BlockSpec((rows, width), lambda i, r=r: (r, 0)) for r in row_at]
    in_specs += [
        pl.BlockSpec((tile, width), lambda i, c=c: (i, c)) for c in range(first, 3)
    ]
    in_specs += [pl.BlockSpec((rows, tile), lambda i: (0, i))] * len(added)
    in_specs += [pl.BlockSpec(memory_space=pl.ANY)] * len(after)
    return pl.pallas_call(
        functools.partial(back_kernel, terms=len(arrays), added=len(added)),
        grid=(width // tile,),
        in_specs=in_specs,
        out_specs=pl.BlockSpec((rows, tile), lambda i: (0, i)),
        out_shape=jax.ShapeDtypeStruct((rows, width), kind),
        compiler_params=pltpu.CompilerParams(vmem_limit_bytes=58 * 1024 * 1024),
        cost_estimate=pl.CostEstimate(
            flops=2 * rows * width * width * len(arrays),
            bytes_accessed=8 * 1024 * 1024,
            transcendentals=0,
        ),
        name="back",
    )(*arrays, *([qkv_weight] * len(arrays)), *added, *after)


def on_device(tokens, qkv_weight, out_grad):
    width = tokens.shape[1]
    low = jnp.bfloat16
    next_one = passed_along(tokens, "ctx", -1)
    next_two = passed_along(next_one, "ctx", -1)
    xs = (tokens, next_one, next_two)
    query = (
        jnp.dot(tokens, qkv_weight[:, :width], preferred_element_type=jnp.float32)
        * (SCALE * LOG2E)
    ).astype(low)
    kvs = [
        jnp.dot(x, qkv_weight[:, width:], preferred_element_type=jnp.float32).astype(low)
        for x in xs
    ]
    bits = []
    while 2 ** len(bits) < lax.axis_size("ctx"):
        bits.append(2 ** len(bits))
    carry = ()
    sums = []
    done = []

    def advance():
        for i in range(len(sums)):
            if done[i] < len(bits):
                sums[i] = exchange(sums[i], "ctx", bits[done[i]])
                done[i] += 1

    for chunk in range(width // SPAN):
        fresh = list(sums)
        *carry, wg = attend_call(chunk, query, out_grad, kvs, xs, carry, fresh)
        advance()
        sums.append(wg)
        done.append(0)
    sums[-1] = exchange(sums[-1], "ctx", bits[0])
    done[-1] = 1
    far = back_call(2, *carry, qkv_weight, low, (), ())
    moved = passed_along(far, "ctx", 1)
    sums[:] = lax.optimization_barrier((far, *sums))[1:]
    advance()
    mid = back_call(1, *carry, qkv_weight, low, (moved,), ())
    moved = passed_along(mid, "ctx", 1)
    sums[:] = lax.optimization_barrier((mid, *sums))[1:]
    own = back_call(0, *carry, qkv_weight, jnp.float32, (), (far,))
    token_grad = (moved.astype(jnp.float32) + own).astype(low)
    late = jnp.concatenate(sums[-2:], axis=1)
    for bit in bits[done[-1]:]:
        late = exchange(late, "ctx", bit)
    sums[-2:] = [late[:, :3 * SPAN], late[:, 3 * SPAN:]]
    done[-2:] = [len(bits)] * 2
    while min(done) < len(bits):
        advance()
    parts = sums
    weight_grad = jnp.concatenate(
        [p[:, i * SPAN:(i + 1) * SPAN] for i in range(3) for p in parts], axis=1
    )
    return (token_grad, weight_grad)


def solution(mesh):
    in_specs = (P(("groups", "ctx"), None), P("groups", None), P(("groups", "ctx"), None))
    out_specs = (P(("groups", "ctx"), None), P(("groups", "ctx"), None))
    return jax.shard_map(
        on_device, mesh=mesh, in_specs=in_specs, out_specs=out_specs, check_vma=False
    )
```
